32 devices in a mesh: tm: 4 (over x, core), height: 2 (over y), fsdp: 4 (over z).
Axes of the slice: x: 2, y: 2, z: 4, core: 2. Of those that a mesh axis runs over, the one named last changes fastest.
Arguments:
- query_primal: bfloat16 [4, 16, 8, 8, 1536], P('fsdp', 'tm', 'height'), may hold values from -125 to 125
- key_primal: bfloat16 [4, 16, 8, 8, 1536], P('fsdp', 'tm', 'height'), may hold values from -5 to 5
- value_primal: bfloat16 [4, 16, 8, 8, 1536], P('fsdp', 'tm', 'height'), may hold values from -6 to 6
- query_tangent: bfloat16 [4, 16, 8, 8, 1536], P('fsdp', 'tm', 'height'), may hold values from -6 to 6
- key_tangent: bfloat16 [4, 16, 8, 8, 1536], P('fsdp', 'tm', 'height'), may hold values from -6 to 6
- value_tangent: bfloat16 [4, 16, 8, 8, 1536], P('fsdp', 'tm', 'height'), may hold values from -6 to 6
- out_weight: bfloat16 [1536, 1536], P(None, ('height', 'fsdp')), may hold values from -0.15625 to 0.15625
- gate_table: float32 [64, 1536], replicated, may hold values from 0.5 to 1.5
- gate_slope: float32 [64, 1536], replicated, may hold values from -4 to 4
- timestep: int32 [4], P('fsdp'), may hold values from 0 to 63
Outputs:
- output_primal: bfloat16 [4, 16, 8, 8, 1536], P('fsdp', 'tm', 'height')
- output_tangent: bfloat16 [4, 16, 8, 8, 1536], P('fsdp', 'tm', 'height')
The draws below stay inside these ranges and needn't reach their ends.
All inputs are finite; a program needn't handle non-finite values.
Results may differ from the reference program's by a relative error of at most 0.008.
Values may be sent and summed in bfloat16 or wider, within the bound.
No kernel may reach another device: no remote copies, remote signals or barrier semaphores. Data moves between devices by JAX's collectives and lax.ppermute only.
A program may use at most 64 MiB of HBM per device.

```python
import math
import jax
import jax.numpy as jnp
from jax import lax

HEADS = 12
HD = 128
DOUT = 1536
TF = 4
TR = 8
COLS = 8
STEPS = 64
BATCH = 4
FRAMES = 16
ROWS = 8


def query_key_pair(key):
    dims_all = (BATCH * FRAMES * ROWS * COLS, HEADS * HD)
    queries = jnp.clip(jax.random.normal(jax.random.fold_in(key, 101), dims_all, jnp.float32), -4.0, 4.0)
    key_draw = jnp.clip(jax.random.normal(jax.random.fold_in(key, 102), dims_all, jnp.float32), -4.0, 4.0)
    full = (BATCH, FRAMES, ROWS, COLS, HEADS * HD)
    return (queries.reshape(full), key_draw.reshape(full))


def draw_query_primal(key, part):
    return query_key_pair(key)[0].astype(jnp.bfloat16)


def draw_key_primal(key, part):
    return query_key_pair(key)[1].astype(jnp.bfloat16)


def place_ends(result, rng, least, top_value):
    shape = result.shape
    spot = [jax.random.randint(jax.random.fold_in(rng, axis), (), 0, shape[axis]) for axis in range(len(shape))]
    result = result.at[tuple(spot)].set(least)
    longest = shape.index(max(shape))
    spot[longest] = (spot[longest] + 1) % shape[longest]
    return result.at[tuple(spot)].set(top_value)


def steps_of(stream_key, extent, split, low, high):
    gain = 1.0
    for axis_at, parts in split:
        draws = jax.random.uniform(jax.random.fold_in(jax.random.fold_in(stream_key, 6), axis_at), (parts,), jnp.float32, low / len(split), high / len(split))
        gain = gain * jnp.repeat(jnp.exp(draws), extent[axis_at] // parts).reshape((-1,) + (1,) * (len(extent) - 1 - axis_at))
    return gain


def gaussian(stream_key, shape, deviation, reach, cuts=(), held_as=jnp.bfloat16):
    values = jax.random.normal(stream_key, shape, jnp.float32) * deviation
    if len(cuts) > 0:
        values = steps_of(stream_key, shape, cuts, -0.22, 0.18) * values
    return jnp.clip(values, min=-reach, max=reach).astype(held_as)


def setup_inputs(seed: int = 0) -> dict:
    streams_of = jax.random.split(jax.random.key(seed), 11)
    query_primal = draw_query_primal(jax.random.fold_in(streams_of[10], 71), 0)
    key_primal = draw_key_primal(jax.random.fold_in(streams_of[10], 71), 0)
    value_primal = gaussian(streams_of[2], (BATCH, FRAMES, ROWS, COLS, HEADS * HD), 1.0, 6.0, ((0, 4), (1, 4), (2, 2)))
    query_tangent = gaussian(streams_of[3], (BATCH, FRAMES, ROWS, COLS, HEADS * HD), 1.0, 6.0, ((0, 4), (1, 4), (2, 2)))
    key_tangent = gaussian(streams_of[4], (BATCH, FRAMES, ROWS, COLS, HEADS * HD), 1.0, 6.0, ((0, 4), (1, 4), (2, 2)))
    value_tangent = gaussian(streams_of[5], (BATCH, FRAMES, ROWS, COLS, HEADS * HD), 1.0, 6.0, ((0, 4), (1, 4), (2, 2)))
    out_weight = gaussian(streams_of[6], (HEADS * HD, DOUT), (HEADS * HD) ** -0.5, 0.15625, ((1, 8),))
    gate_table = jnp.clip(jax.random.uniform(streams_of[7], (STEPS, DOUT), jnp.float32, 0.5, 1.5), 0.5, 1.5)
    gate_slope = gaussian(streams_of[8], (STEPS, DOUT), 1.0, 4.0, (), jnp.float32)
    timestep = place_ends(jax.random.randint(streams_of[9], (BATCH,), 0, STEPS), jax.random.fold_in(streams_of[9], 1), 0, STEPS - 1).astype(jnp.int32)
    return {"query_primal": query_primal, "key_primal": key_primal, "value_primal": value_primal, "query_tangent": query_tangent, "key_tangent": key_tangent, "value_tangent": value_tangent, "out_weight": out_weight, "gate_table": gate_table, "gate_slope": gate_slope, "timestep": timestep}


def attend(queries, keys_all, values_all, queries_t, keys_t, values_t, allowed):
    scaling = 1.0 / math.sqrt(queries.shape[-1])
    query_f = queries.astype(jnp.float32)
    key_f = keys_all.astype(jnp.float32)
    scores = jnp.einsum('qhd,khd->hqk', query_f, key_f) * scaling
    scores = jnp.where(allowed[None], scores, -1e+30)
    row_max = lax.optimization_barrier(jnp.max(scores, axis=-1, keepdims=True))
    lifted = jnp.exp(scores - row_max)
    probs = lifted / lax.optimization_barrier(jnp.sum(lifted, axis=-1, keepdims=True))
    probs_low = probs.astype(jnp.bfloat16)
    primal = jnp.einsum('hqk,khd->qhd', probs_low.astype(jnp.float32), values_all.astype(jnp.float32))
    slopes = (jnp.einsum('qhd,khd->hqk', queries_t.astype(jnp.float32), key_f) + jnp.einsum('qhd,khd->hqk', query_f, keys_t.astype(jnp.float32))) * scaling
    centre = lax.optimization_barrier(jnp.sum(probs * slopes, axis=-1, keepdims=True))
    weights_t = (probs * (slopes - centre)).astype(jnp.bfloat16)
    tangent = jnp.einsum('hqk,khd->qhd', weights_t.astype(jnp.float32), values_all.astype(jnp.float32)) + jnp.einsum('hqk,khd->qhd', probs_low.astype(jnp.float32), values_t.astype(jnp.float32))
    return (primal.astype(jnp.bfloat16), tangent.astype(jnp.bfloat16))

def reference(query_primal, key_primal, value_primal, query_tangent, key_tangent, value_tangent, out_weight, gate_table, gate_slope, timestep):
    batches, frames, rows, columns, features = query_primal.shape
    head_count = features // HD
    time_tiles = frames // TF
    row_tiles = rows // TR
    widths = ((0, 0), (1, 1), (0, 0), (0, 0), (0, 0))
    padded = [jnp.pad(array, widths) for array in (key_primal, value_primal, key_tangent, value_tangent)]
    ext_frames = TF + 2
    frame_ids = lax.broadcasted_iota(jnp.int32, (ext_frames, TR, columns), 0).reshape(-1)
    zero_idx = jnp.zeros((), jnp.int32)

    def one_tile(tile_id):
        batch_id = (tile_id // (time_tiles * row_tiles)).astype(jnp.int32)
        time_id = (tile_id // row_tiles % time_tiles).astype(jnp.int32)
        row_id = (tile_id % row_tiles).astype(jnp.int32)
        first_frame = (time_id * TF).astype(jnp.int32)
        first_row = (row_id * TR).astype(jnp.int32)

        def cut(array, length):
            block = lax.dynamic_slice(array, (batch_id, first_frame, first_row, zero_idx, zero_idx), (1, length, TR, columns, features))
            return block.reshape(-1, head_count, HD)
        global_frame = first_frame + frame_ids - 1
        inside = (global_frame >= 0) & (global_frame < frames)
        allowed = inside[None, :]
        primal, tangent = attend(cut(query_primal, TF), cut(padded[0], ext_frames), cut(padded[1], ext_frames), cut(query_tangent, TF), cut(padded[2], ext_frames), cut(padded[3], ext_frames), allowed)
        return (primal.reshape(TF, TR, columns, features), tangent.reshape(TF, TR, columns, features))
    tile_total = batches * time_tiles * row_tiles
    primal_tiles, tangent_tiles = lax.map(one_tile, jnp.arange(tile_total, dtype=jnp.int32))

    def arrange(tiles):
        tiles = tiles.reshape(batches, time_tiles, row_tiles, TF, TR, columns, features)
        return tiles.transpose(0, 1, 3, 2, 4, 5, 6).reshape(batches, frames, rows, columns, features)
    attn_primal = arrange(primal_tiles)
    attn_tangent = arrange(tangent_tiles)

    def project_batch(batch_id):
        flat_p = lax.dynamic_index_in_dim(attn_primal, batch_id, 0, keepdims=False).reshape(-1, features)
        flat_t = lax.dynamic_index_in_dim(attn_tangent, batch_id, 0, keepdims=False).reshape(-1, features)
        projected = jnp.dot(flat_p, out_weight, preferred_element_type=jnp.float32)
        projected_t = jnp.dot(flat_t, out_weight, preferred_element_type=jnp.float32)
        step_id = lax.dynamic_index_in_dim(timestep, batch_id, 0, keepdims=False).astype(jnp.int32)
        gate_row = lax.dynamic_index_in_dim(gate_table, step_id, 0, keepdims=False)
        slope_row = lax.dynamic_index_in_dim(gate_slope, step_id, 0, keepdims=False)
        out_p = (gate_row * projected).astype(jnp.bfloat16)
        out_t = (gate_row * projected_t + slope_row * projected).astype(jnp.bfloat16)
        return (out_p, out_t)
    outs_p, outs_t = lax.map(project_batch, jnp.arange(batches, dtype=jnp.int32))
    dout = out_weight.shape[1]
    return (outs_p.reshape(batches, frames, rows, columns, dout), outs_t.reshape(batches, frames, rows, columns, dout))
```

```python
import functools
import math

import jax
import jax.numpy as jnp
from jax import lax
from jax.experimental import pallas as pl
from jax.experimental.pallas import tpu as pltpu
from jax.sharding import PartitionSpec as P

HD = 128
LOG2E = 1.4426950408889634
VMEM_LIMIT = 40 * 1024 * 1024


def swap(value, axis, mask):
    pairs = [(source, source ^ mask) for source in range(lax.axis_size(axis))]
    return lax.ppermute(value, axis, pairs)


def swap_odd(value, axis):
    pairs = []
    for low in range(1, lax.axis_size(axis) - 1, 2):
        pairs += [(low, low + 1), (low + 1, low)]
    return lax.ppermute(value, axis, pairs)


def dot_nt(a, b):
    return lax.dot_general(a, b, (((1,), (1,)), ((), ())), preferred_element_type=jnp.float32)


def score_kernel(mask, q, qt, k_own, kt_own, k_par, kt_par, k_a, k_b, p_out, w_out):
    tokens, features = q.shape
    half = k_a.shape[0] // 2
    edge = half // 2
    scaling = 1.0 / math.sqrt(HD)
    allowed = mask[...] > 0.0
    for head in range(features // HD):
        at = pl.ds(head * HD, HD)

        def ordered(own, par, at_halo):
            return jnp.concatenate(
                [
                    own[:, at],
                    par[pl.ds(0, edge), at],
                    par[pl.ds(tokens - edge, edge), at],
                    k_a[at_halo, at],
                    k_b[at_halo, at],
                    par[pl.ds(edge, tokens - 2 * edge), at],
                ],
                0,
            )

        keys = ordered(k_own, k_par, pl.ds(0, half))
        keys_t = ordered(kt_own, kt_par, pl.ds(half, half))
        query, query_t = q[:, at], qt[:, at]
        raw = jnp.where(allowed, dot_nt(query, keys), -1e30)
        top = jnp.max(raw, axis=-1, keepdims=True)
        lifted = jnp.exp2((raw - top) * (scaling * LOG2E))
        probs = lifted * (1.0 / jnp.sum(lifted, axis=-1, keepdims=True))
        slopes = scaling * dot_nt(
            jnp.concatenate([query_t, query], 1), jnp.concatenate([keys, keys_t], 1)
        )
        centre = jnp.sum(probs * slopes, axis=-1, keepdims=True)
        p_out[head] = probs.astype(jnp.bfloat16)
        w_out[head] = (probs * (slopes - centre)).astype(jnp.bfloat16)


def scores(mask, *arrays):
    tokens, features = arrays[0].shape
    heads = features // HD
    keys = mask.shape[1]
    out = jax.ShapeDtypeStruct((heads, tokens, keys), jnp.bfloat16)
    return pl.pallas_call(
        score_kernel,
        out_shape=(out, out),
        compiler_params=pltpu.CompilerParams(vmem_limit_bytes=VMEM_LIMIT),
        cost_estimate=pl.CostEstimate(
            flops=6 * heads * tokens * keys * HD, bytes_accessed=6_000_000, transcendentals=heads * tokens * keys
        ),
        name="scores",
    )(mask, *arrays)


def project_kernel(layout, step, places, gate, slope, p, w, v_own, vt_own, v_edge, v_mid, v_a, v_b, *rest):
    pieces = rest[: len(layout)]
    out_p, out_t, weight, attn, sems = rest[len(layout) :]
    tokens = v_own.shape[0]
    half = v_a.shape[0] // 2
    copies = []
    unit_at = 0
    for piece, (units, rows) in zip(pieces, layout):
        for unit in range(units):
            start = pl.multiple_of(places[unit_at] * 16, 16)
            copies.append(
                pltpu.make_async_copy(
                    piece.at[pl.ds(unit * rows, rows), :], weight.at[pl.ds(start, rows), :], sems.at[unit_at]
                )
            )
            unit_at += 1
    for copy in copies:
        copy.start()
    for head in range(p.shape[0]):
        at = pl.ds(head * HD, HD)

        def ordered(own, rows):
            return jnp.concatenate([own[:, at], v_edge[rows, at], v_a[rows, at], v_b[rows, at], v_mid[rows, at]], 0)

        values = ordered(v_own, pl.ds(0, half))
        values_t = ordered(vt_own, pl.ds(half, half))
        probs = p[head]
        primal = jnp.dot(probs, values, preferred_element_type=jnp.float32)
        tangent = jnp.dot(
            jnp.concatenate([w[head], probs], 1),
            jnp.concatenate([values, values_t], 0),
            preferred_element_type=jnp.float32,
        )
        attn[pl.ds(0, tokens), at] = primal.astype(jnp.bfloat16)
        attn[pl.ds(tokens, tokens), at] = tangent.astype(jnp.bfloat16)
    for copy in copies:
        copy.wait()
    row = pl.ds(step[0] % 8, 1)
    width = 256
    for first in range(0, weight.shape[0], width):
        cols = pl.ds(first, width)
        both = dot_nt(attn[...], weight[cols, :])
        main, main_t = both[:tokens], both[tokens:]
        gate_row, slope_row = gate[row, cols], slope[row, cols]
        out_p[:, cols] = (gate_row * main).astype(jnp.bfloat16)
        out_t[:, cols] = (gate_row * main_t + slope_row * main).astype(jnp.bfloat16)


def project(step, places, gate_table, gate_slope, probs, weights_t, values, pieces, layout):
    tokens, features = values[0].shape
    dout = gate_table.shape[1]
    units = places.shape[0]
    out = jax.ShapeDtypeStruct((tokens, dout), jnp.bfloat16)
    whole = lambda a: pl.BlockSpec(a.shape, lambda i, *_: (0,) * a.ndim)
    table = pl.BlockSpec((8, dout), lambda i, step, places: (step[0] // 8, 0))
    return pl.pallas_call(
        functools.partial(project_kernel, layout),
        out_shape=(out, out),
        grid_spec=pltpu.PrefetchScalarGridSpec(
            num_scalar_prefetch=2,
            grid=(1,),
            in_specs=[table, table, whole(probs), whole(weights_t)]
            + [whole(v) for v in values]
            + [pl.BlockSpec(memory_space=pl.ANY)] * len(pieces),
            out_specs=(whole(out), whole(out)),
            scratch_shapes=[
                pltpu.VMEM((dout, features), jnp.bfloat16),
                pltpu.VMEM((2 * tokens, features), jnp.bfloat16),
                pltpu.SemaphoreType.DMA((units,)),
            ],
        ),
        compiler_params=pltpu.CompilerParams(vmem_limit_bytes=VMEM_LIMIT),
        cost_estimate=pl.CostEstimate(
            flops=4 * tokens * features * dout, bytes_accessed=10_000_000, transcendentals=0
        ),
        name="project",
    )(step, places, gate_table, gate_slope, probs, weights_t, *values, *pieces)


def gather_weight(block):
    columns = block.shape[0]
    tm, height, fsdp = (lax.axis_size(axis) for axis in ("tm", "height", "fsdp"))
    rows = columns // 4
    if (tm % 4, height, fsdp) != (0, 2, 4) or rows % 16 != 0:
        full = lax.all_gather(block, ("height", "fsdp"), axis=0, tiled=True)
        return [full], [(1, full.shape[0])], jnp.zeros((1,), jnp.int32)
    mine = lax.axis_index("tm") % 4
    h, f = lax.axis_index("height"), lax.axis_index("fsdp")
    quarter = lax.dynamic_slice_in_dim(block, mine * rows, rows, 0)
    other = swap(quarter, "height", 1)
    own3 = swap(quarter, "fsdp", 3)
    own2 = swap(quarter, "fsdp", 2)
    both1 = swap(jnp.concatenate([quarter, other], 0), "fsdp", 1)
    other3 = swap(other, "fsdp", 3)
    other2 = swap(other, "fsdp", 2)
    held_a = jnp.concatenate([other, own3], 0)
    cross_a = swap(held_a, "tm", 2)
    held_b = jnp.concatenate([both1, own2], 0)
    cross_b = swap(held_b, "tm", 2)
    held_c = jnp.concatenate([other3, other2], 0)
    cross_c = swap(held_c, "tm", 2)
    first = jnp.concatenate([held_a, held_b, cross_a, cross_b], 0)
    second = jnp.concatenate([held_c, cross_c], 0)
    near_first = swap(first, "tm", 1)
    near_second = swap(second, "tm", 1)
    in_a, in_b, in_c = [(1, 0), (0, 3)], [(0, 1), (1, 1), (0, 2)], [(1, 3), (1, 2)]

    def place(kinds, mask):
        return [((((h ^ dh) * fsdp + (f ^ df)) * 4 + (mine ^ mask)) * rows) // 16 for dh, df in kinds]

    spots = [((h * fsdp + f) * columns) // 16]
    for mask in (0, 1):
        spots += place(in_a + in_b, mask) + place(in_a + in_b, mask ^ 2)
    for mask in (0, 1):
        spots += place(in_c, mask) + place(in_c, mask ^ 2)
    pieces = [block, first, near_first, second, near_second]
    layout = [(1, columns), (10, rows), (10, rows), (4, rows), (4, rows)]
    return pieces, layout, jnp.stack(spots).astype(jnp.int32)


def local(
    query_primal,
    key_primal,
    value_primal,
    query_tangent,
    key_tangent,
    value_tangent,
    out_weight,
    gate_table,
    gate_slope,
    timestep,
):
    _, frames, rows, columns, features = query_primal.shape
    per_frame = rows * columns
    tokens = frames * per_frame
    flat = lambda x: x.reshape(tokens, features)
    q, qt, k, kt, v, vt = map(
        flat, (query_primal, query_tangent, key_primal, key_tangent, value_primal, value_tangent)
    )
    last = tokens - per_frame
    pieces, layout, places = gather_weight(out_weight.T)
    k_par = swap(k, "height", 1)
    kt_par = swap(kt, "height", 1)
    v_edge = swap(
        jnp.concatenate([v[:per_frame], v[last:], vt[:per_frame], vt[last:]], 0), "height", 1
    )
    v_mid = swap(jnp.concatenate([v[per_frame:last], vt[per_frame:last]], 0), "height", 1)
    tm = lax.axis_index("tm")
    even = tm % 2 == 0

    def end(array, from_last):
        start = jnp.where(from_last, array.shape[0] - per_frame, 0)
        return lax.dynamic_slice_in_dim(array, start, per_frame, 0)

    def halo(own, par, own_t, par_t):
        to_a = jnp.concatenate([end(a, even) for a in (own, par, own_t, par_t)], 0)
        to_b = jnp.concatenate([end(a, ~even) for a in (own, par, own_t, par_t)], 0)
        return swap(to_a, "tm", 1), swap_odd(to_b, "tm")

    k_a, k_b = halo(k, k_par, kt, kt_par)
    v_a, v_b = halo(v, v_edge[: 2 * per_frame], vt, v_edge[2 * per_frame :])
    inside = (tm > 0) & (tm < lax.axis_size("tm") - 1)
    spot = lax.broadcasted_iota(jnp.int32, (1, 2 * tokens + 4 * per_frame), 1)
    b_start = tokens + 4 * per_frame
    is_b = (spot >= b_start) & (spot < b_start + 2 * per_frame)
    mask = jnp.where(is_b & ~inside, 0.0, 1.0)
    probs, weights_t = scores(mask, q, qt, k, kt, k_par, kt_par, k_a, k_b)
    out_p, out_t = project(
        timestep, places, gate_table, gate_slope, probs, weights_t, (v, vt, v_edge, v_mid, v_a, v_b), pieces, layout
    )
    shape = query_primal.shape[:-1] + (out_p.shape[1],)
    return out_p.reshape(shape), out_t.reshape(shape)


def solution(mesh):
    token_spec = P("fsdp", "tm", "height", None, None)
    in_specs = (token_spec,) * 6 + (P(None, ("height", "fsdp")), P(), P(), P("fsdp"))
    return jax.shard_map(
        local, mesh=mesh, in_specs=in_specs, out_specs=(token_spec, token_spec), check_vma=False
    )
```

```python
import math

import jax
import jax.numpy as jnp
from jax import lax
from jax.experimental import pallas as pl
from jax.experimental.pallas import tpu as pltpu
from jax.sharding import PartitionSpec as P

HD = 128
ORDER = {
    "k_par": ["own"],
    "twos": ["own_parts"],
    "half": ["own_parts"],
    "threes": ["k_par"],
    "cross": ["near_b"],
    "v_mid": ["threes"],
    "near": ["v_mid"],
    "gates": ["twos"],
    "late_parts": ["threes"],
}
LOG2E = 1.4426950408889634
VMEM_LIMIT = 24 * 1024 * 1024
SMALL = pl.CostEstimate(flops=1, bytes_accessed=1, transcendentals=0)
SCORES_COST = pl.CostEstimate(flops=20_000_000_000, bytes_accessed=1, transcendentals=0)


def swap(value, axis, mask):
    pairs = [(source, source ^ mask) for source in range(lax.axis_size(axis))]
    return lax.ppermute(value, axis, pairs)


def swap_odd(value, axis):
    pairs = []
    for low in range(1, lax.axis_size(axis) - 1, 2):
        pairs += [(low, low + 1), (low + 1, low)]
    return lax.ppermute(value, axis, pairs)


def dot_nt(a, b):
    return lax.dot_general(a, b, (((1,), (1,)), ((), ())), preferred_element_type=jnp.float32)


def after(value, *done):
    return lax.optimization_barrier((value,) + done)[0]


def gather_rows(name, outs, moves, sources, limit=VMEM_LIMIT):
    features = sources[0].shape[1]

    def kernel(*refs):
        even = lax.axis_index("tm") & 1 == 0
        ins, rest, sems = refs[: len(sources)], refs[len(sources) : -1], refs[-1]
        copies = []
        for i, (source, row, out, to, count) in enumerate(moves):
            if isinstance(row, tuple):
                row = pl.multiple_of(jnp.where(even, *row), 16)
            copies.append(
                pltpu.make_async_copy(
                    ins[source].at[pl.ds(row, count), :], rest[out].at[pl.ds(to, count), :], sems.at[i]
                )
            )
        for copy in copies:
            copy.start()
        for copy in copies:
            copy.wait()

    return pl.pallas_call(
        kernel,
        out_shape=[jax.ShapeDtypeStruct((n, features), sources[0].dtype) for n in outs],
        in_specs=[pl.BlockSpec(memory_space=pl.ANY)] * len(sources),
        out_specs=[pl.BlockSpec(memory_space=pltpu.VMEM)] * len(outs),
        scratch_shapes=[pltpu.SemaphoreType.DMA((len(moves),))],
        compiler_params=pltpu.CompilerParams(vmem_limit_bytes=limit),
        cost_estimate=SMALL,
        name=name,
    )(*sources)


def table_rows(step, gate_table, gate_slope):
    features = gate_table.shape[1]

    def kernel(step, gate, slope, gate_row, slope_row):
        row = pl.ds(step[0] & 7, 1)
        gate_row[...] = gate[row, :]
        slope_row[...] = slope[row, :]

    table = pl.BlockSpec((8, features), lambda i, step: (step[0] >> 3, 0))
    one = pl.BlockSpec((1, features), lambda i, step: (0, 0))
    return pl.pallas_call(
        kernel,
        out_shape=[jax.ShapeDtypeStruct((1, features), gate_table.dtype)] * 2,
        grid_spec=pltpu.PrefetchScalarGridSpec(
            num_scalar_prefetch=1, grid=(1,), in_specs=[table, table], out_specs=[one, one]
        ),
        compiler_params=pltpu.CompilerParams(vmem_limit_bytes=VMEM_LIMIT),
        cost_estimate=SMALL,
        name="table_rows",
    )(step, gate_table, gate_slope)


def score_kernel(q, qt, k, kt, k_par, par, near_a, near_b, late_a, late_b, p_out, w_out, mid_out):
    tokens, features = q.shape
    edge = near_a.shape[0] // 4
    half = 2 * edge
    inner = tokens - 2 * edge
    first = tokens + 2 * half
    scaling = 1.0 / math.sqrt(HD)
    tm = lax.axis_index("tm")
    inside = (tm > 0) & (tm < lax.axis_size("tm") - 1)
    seen = jnp.where(inside, tokens + 2 * half + inner + half, tokens + 2 * half + inner)
    allowed = lax.broadcasted_iota(jnp.int32, (tokens, 2 * tokens + 2 * half), 1) < seen
    for head in range(features // HD):
        at = pl.ds(head * HD, HD)

        def ordered(own, par, i):
            rows = pl.ds(i * edge, edge)
            return jnp.concatenate(
                [
                    own[:, at],
                    par[pl.ds(0, edge), at],
                    par[pl.ds(tokens - edge, edge), at],
                    near_a[rows, at],
                    late_a[rows, at],
                    par[pl.ds(edge, inner), at],
                    near_b[rows, at],
                    late_b[rows, at],
                ],
                0,
            )

        keys, keys_t = ordered(k, k_par, 0), ordered(kt, par, 1)
        query, query_t = q[:, at], qt[:, at]
        raw = jnp.where(allowed, dot_nt(query, keys), -1e30)
        top = jnp.max(raw, axis=-1, keepdims=True)
        lifted = jnp.exp2((raw - top) * (scaling * LOG2E))
        probs = lifted * (1.0 / jnp.sum(lifted, axis=-1, keepdims=True))
        slopes = scaling * dot_nt(
            jnp.concatenate([query_t, query], 1), jnp.concatenate([keys, keys_t], 1)
        )
        centre = jnp.sum(probs * slopes, axis=-1, keepdims=True)
        probs_low = probs.astype(jnp.bfloat16)
        weights_t = (probs * (slopes - centre)).astype(jnp.bfloat16)
        p_out[head] = probs_low
        w_out[head] = weights_t
        part = probs_low[:, first : first + inner]
        mid_out[head, pl.ds(0, tokens), :] = jnp.concatenate([part, jnp.zeros_like(part)], 1)
        mid_out[head, pl.ds(tokens, tokens), :] = jnp.concatenate([weights_t[:, first : first + inner], part], 1)


def scores(*arrays):
    tokens, features = arrays[0].shape
    heads = features // HD
    keys = 2 * tokens + arrays[-1].shape[0]
    inner = tokens - arrays[-1].shape[0] // 2
    out = jax.ShapeDtypeStruct((heads, tokens, keys), jnp.bfloat16)
    mid = jax.ShapeDtypeStruct((heads, 2 * tokens, 2 * inner), jnp.bfloat16)
    return pl.pallas_call(
        score_kernel,
        out_shape=(out, out, mid),
        in_specs=[pl.BlockSpec(memory_space=pltpu.VMEM)] * len(arrays),
        out_specs=[pl.BlockSpec(memory_space=pltpu.VMEM)] * 3,
        compiler_params=pltpu.CompilerParams(vmem_limit_bytes=VMEM_LIMIT),
        cost_estimate=SCORES_COST,
        name="scores",
    )(*arrays)


def values_kernel(layout, p, w, own, mids, par, near_a, near_b, late_a, late_b, *rest):
    pieces = rest[: len(layout)]
    total, weight = rest[len(layout) :]
    tokens = p.shape[1]
    edge = near_a.shape[0] // 4
    half, inner = 2 * edge, tokens - 2 * edge
    tm, h, f = (lax.axis_index(axis) for axis in ("tm", "height", "fsdp"))
    for piece, (units, rows) in zip(pieces, layout):
        for i, unit in enumerate(units):
            start = 0
            if unit is not None:
                dh, df, dq = unit
                wide = weight.shape[0] // (lax.axis_size("height") * lax.axis_size("fsdp"))
                start = ((h ^ dh) * lax.axis_size("fsdp") + (f ^ df)) * wide
                if dq is not None:
                    start = start + ((tm & 3) ^ dq) * rows
                start = pl.multiple_of(start, 16)
            weight[pl.ds(start, rows), :] = piece[pl.ds(i * rows, rows), :]
    gap = jnp.zeros((inner, HD), jnp.bfloat16)
    for head in range(p.shape[0]):
        at = pl.ds(head * HD, HD)

        def ordered(i):
            halo = pl.ds(half + i * edge, edge)
            base = tokens + i * half
            return jnp.concatenate(
                [
                    own[pl.ds(base, edge), at],
                    mids[pl.ds(i * inner, inner), at],
                    own[pl.ds(base + edge, edge), at],
                    par[pl.ds(base, half), at],
                    near_a[halo, at],
                    late_a[halo, at],
                    gap,
                    near_b[halo, at],
                    late_b[halo, at],
                ],
                0,
            )

        values, values_t = ordered(0), ordered(1)
        probs = p[head]
        total[pl.ds(0, tokens), at] = jnp.dot(probs, values, preferred_element_type=jnp.float32)
        total[pl.ds(tokens, tokens), at] = jnp.dot(
            jnp.concatenate([w[head], probs], 1),
            jnp.concatenate([values, values_t], 0),
            preferred_element_type=jnp.float32,
        )


def values_known(probs, weights_t, values, pieces, layout, dout):
    tokens, features = probs.shape[1], values[0].shape[1]
    arrays = (probs, weights_t, *values, *pieces)
    return pl.pallas_call(
        lambda *refs: values_kernel(layout, *refs),
        out_shape=(
            jax.ShapeDtypeStruct((2 * tokens, features), jnp.float32),
            jax.ShapeDtypeStruct((dout, features), jnp.bfloat16),
        ),
        in_specs=[pl.BlockSpec(memory_space=pltpu.VMEM)] * len(arrays),
        out_specs=[pl.BlockSpec(memory_space=pltpu.VMEM)] * 2,
        compiler_params=pltpu.CompilerParams(vmem_limit_bytes=VMEM_LIMIT),
        cost_estimate=SMALL,
        name="values",
    )(*arrays)


def project_kernel(gate, slope, mid, total, weight, v_mid, out_p, out_t, attn):
    tokens = out_p.shape[0]
    for head in range(mid.shape[0]):
        at = pl.ds(head * HD, HD)
        rest = jnp.dot(mid[head], v_mid[:, at], preferred_element_type=jnp.float32)
        attn[:, at] = (total[:, at] + rest).astype(jnp.bfloat16)
    width = 256
    for first in range(0, weight.shape[0], width):
        cols = pl.ds(first, width)
        both = dot_nt(attn[...], weight[cols, :])
        main, main_t = both[:tokens], both[tokens:]
        gate_row, slope_row = gate[:, cols], slope[:, cols]
        out_p[:, cols] = (gate_row * main).astype(jnp.bfloat16)
        out_t[:, cols] = (gate_row * main_t + slope_row * main).astype(jnp.bfloat16)


def project(gate, slope, mid, total, weight, v_mid):
    rows, features = total.shape
    dout = weight.shape[0]
    out = jax.ShapeDtypeStruct((rows // 2, dout), jnp.bfloat16)
    return pl.pallas_call(
        project_kernel,
        out_shape=(out, out),
        in_specs=[pl.BlockSpec(memory_space=pltpu.VMEM)] * 6,
        scratch_shapes=[pltpu.VMEM((rows, features), jnp.bfloat16)],
        compiler_params=pltpu.CompilerParams(vmem_limit_bytes=VMEM_LIMIT),
        cost_estimate=SMALL,
        name="project",
    )(gate, slope, mid, total, weight, v_mid)


def local(
    query_primal,
    key_primal,
    value_primal,
    query_tangent,
    key_tangent,
    value_tangent,
    out_weight,
    gate_table,
    gate_slope,
    timestep,
):
    _, frames, rows, columns, features = query_primal.shape
    per_frame = rows * columns
    tokens = frames * per_frame
    flat = lambda x: x.reshape(tokens, features)
    q, qt, k, kt, v, vt = map(
        flat, (query_primal, query_tangent, key_primal, key_tangent, value_primal, value_tangent)
    )
    block = out_weight.T
    wide = block.shape[0]
    part = wide // 4
    fsdp = lax.axis_size("fsdp")
    in_quarters = (lax.axis_size("tm") % 4, lax.axis_size("height"), fsdp) == (0, 2, 4) and part % 16 == 0
    two = 2 * per_frame
    inner, last = tokens - two, tokens - per_frame
    ends = ((0, last), (last, 0))

    def own_parts(k, kt, v, vt):
        moves = [(1, 0, 0, 0, tokens)]
        for i, source in ((0, 2), (1, 3)):
            moves.append((source, 0, 0, tokens + i * two, per_frame))
            moves.append((source, last, 0, tokens + i * two + per_frame, per_frame))
            moves.append((source, per_frame, 1, inner * i, inner))
        for out, (odd, even) in ((2, ends[0]), (3, ends[1])):
            for source in range(4):
                moves.append((source, (even, odd), out, source * per_frame, per_frame))
        return gather_rows("own_parts", [tokens + 2 * two, 2 * inner, 2 * two, 2 * two], moves, [k, kt, v, vt], 58 * 1024 * 1024)

    def late_parts(k_par, par):
        moves = []
        for out, (odd, even) in ((0, ends[0]), (1, ends[1])):
            for i in range(2):
                moves.append((i, (even, odd), out, i * per_frame, per_frame))
                row = tuple(tokens + i * two + min(end, per_frame) for end in (even, odd))
                moves.append((1, row, out, (2 + i) * per_frame, per_frame))
        return gather_rows("late_parts", [2 * two, 2 * two], moves, [k_par, par])

    steps = {
        "k": ((), lambda: k),
        "kt": ((), lambda: kt),
        "v": ((), lambda: (v, vt)),
        "own_parts": (("k", "kt", "v"), lambda k, kt, v: own_parts(k, kt, *v)),
        "k_par": (("k",), lambda k: swap(k, "height", 1)),
        "par": (("own_parts",), lambda parts: swap(parts[0], "height", 1)),
        "v_mid": (("own_parts",), lambda parts: swap(parts[1], "height", 1)),
        "near_a": (("own_parts",), lambda parts: swap(parts[2], "tm", 1)),
        "near_b": (("own_parts",), lambda parts: swap_odd(parts[3], "tm")),
        "late_parts": (("k_par", "par"), late_parts),
        "late_a": (("late_parts",), lambda sides: swap(sides[0], "tm", 1)),
        "late_b": (("late_parts",), lambda sides: swap_odd(sides[1], "tm")),
        "scores": (
            ("k_par", "par", "near_a", "near_b", "late_a", "late_b"),
            lambda *arrays: scores(q, qt, k, kt, *arrays),
        ),
        "tables": ((), lambda: (timestep, gate_table, gate_slope)),
        "gates": (("tables",), lambda tables: table_rows(*tables)),
    }
    if in_quarters:
        mine = lax.axis_index("tm") & 3
        quarter = lambda which: lax.dynamic_slice_in_dim(block, which * part, part, 0)
        near = lambda group: [(dh, df, dq ^ 1) for dh, df, dq in group]
        cat = lambda *arrays: jnp.concatenate(arrays, 0)
        steps["own"] = ((), lambda: quarter(mine))
        steps["other"] = (("own",), lambda own: swap(own, "height", 1))
        steps["pair"] = (("own", "other"), cat)
        steps["half"] = (("pair",), lambda pair: cat(quarter(mine ^ 2), pair))
        steps["twos"] = (("pair",), lambda pair: swap(pair, "fsdp", 2))
        steps["ones"] = (("half",), lambda half: swap(half, "fsdp", 1))
        steps["threes"] = (("twos",), lambda twos: swap(twos, "fsdp", 1))
        steps["other_x"] = (("other",), lambda other: swap(other, "tm", 2))
        steps["cross"] = (("ones", "twos"), lambda ones, twos: swap(cat(ones[2 * part :], twos), "tm", 2))
        steps["cross_threes"] = (("threes",), lambda threes: swap(threes, "tm", 2))
        steps["mine"] = (("other", "ones", "twos", "threes", "other_x", "cross", "cross_threes"), cat)
        units = [(1, 0, 0), (0, 1, 2), (0, 1, 0), (1, 1, 0), (0, 2, 0), (1, 2, 0), (0, 3, 0), (1, 3, 0)]
        units += [(1, 0, 2), (1, 1, 2), (0, 2, 2), (1, 2, 2), (0, 3, 2), (1, 3, 2)]
        steps["near"] = (("mine",), lambda mine: swap(mine, "tm", 1))
        pieces = ("mine", "near")
        layout = [([(0, 0, None)], wide), (units, part), (near(units), part)]
        order = ORDER
    else:
        steps["weight"] = ((), lambda: lax.all_gather(block, ("height", "fsdp"), axis=0, tiled=True))
        pieces, layout, order = ("weight",), [([None], gate_table.shape[1])], {}
    known = {}

    def get(name):
        if name not in known:
            takes, make = steps[name]
            arrays = [get(take) for take in takes]
            first = [get(step) for step in order.get(name, ())]
            if first:
                arrays = lax.optimization_barrier((arrays, first))[0]
            known[name] = make(*arrays)
        return known[name]

    probs, weights_t, mid = get("scores")
    own, middle, _, _ = get("own_parts")
    known_values = (own, middle, *(get(name) for name in ("par", "near_a", "near_b", "late_a", "late_b")))
    parts = ([block] if in_quarters else []) + [get(piece) for piece in pieces]
    total, weight = values_known(probs, weights_t, known_values, parts, layout, gate_table.shape[1])
    out_p, out_t = project(*get("gates"), mid, total, weight, get("v_mid"))
    shape = query_primal.shape[:-1] + (out_p.shape[1],)
    return out_p.reshape(shape), out_t.reshape(shape)


def solution(mesh):
    token_spec = P("fsdp", "tm", "height", None, None)
    in_specs = (token_spec,) * 6 + (P(None, ("height", "fsdp")), P(), P(), P("fsdp"))
    return jax.shard_map(
        local, mesh=mesh, in_specs=in_specs, out_specs=(token_spec, token_spec), check_vma=False
    )
```

```python
import math

import jax
import jax.numpy as jnp
from jax import lax
from jax.experimental import pallas as pl
from jax.experimental.pallas import tpu as pltpu
from jax.sharding import PartitionSpec as P

HD = 128
ORDER = {
    "k_par": ["own"],
    "twos": ["own_parts"],
    "threes": ["k_par"],
    "v_mid": ["k_par"],
    "near": ["v_mid"],
    "gates": ["twos"],
    "late_parts": ["threes"],
    "near_b": ["other_x"],
    "near_a": ["near_b"],
}
LOG2E = 1.4426950408889634
VMEM_LIMIT = 24 * 1024 * 1024
SMALL = pl.CostEstimate(flops=1, bytes_accessed=1, transcendentals=0)
SCORES_COST = pl.CostEstimate(flops=20_000_000_000, bytes_accessed=1, transcendentals=0)


def swap(value, axis, mask):
    pairs = [(source, source ^ mask) for source in range(lax.axis_size(axis))]
    return lax.ppermute(value, axis, pairs)


def swap_odd(value, ends_meet):
    tiles, samples = lax.axis_size("tm"), lax.axis_size("fsdp")
    pairs = []
    for tile in range(tiles):
        other = tile + 1 if tile % 2 else tile - 1
        for sample in range(samples):
            target = (other % tiles, sample)
            if not 0 <= other < tiles and not ends_meet:
                target = (tile, sample ^ 1)
            pairs.append((tile * samples + sample, target[0] * samples + target[1]))
    return lax.ppermute(value, ("tm", "fsdp"), pairs)


def swap_odd_alone(value, axis):
    pairs = []
    for low in range(1, lax.axis_size(axis) - 1, 2):
        pairs += [(low, low + 1), (low + 1, low)]
    return lax.ppermute(value, axis, pairs)


def dot_nt(a, b):
    return lax.dot_general(a, b, (((1,), (1,)), ((), ())), preferred_element_type=jnp.float32)


def after(value, *done):
    return lax.optimization_barrier((value,) + done)[0]


def gather_rows(name, outs, moves, sources, limit=VMEM_LIMIT):
    features = sources[0].shape[1]

    def kernel(*refs):
        even = lax.axis_index("tm") & 1 == 0
        ins, rest, sems = refs[: len(sources)], refs[len(sources) : -1], refs[-1]
        copies = []
        for i, (source, row, out, to, count) in enumerate(moves):
            if isinstance(row, tuple):
                row = pl.multiple_of(jnp.where(even, *row), 16)
            copies.append(
                pltpu.make_async_copy(
                    ins[source].at[pl.ds(row, count), :], rest[out].at[pl.ds(to, count), :], sems.at[i]
                )
            )
        for copy in copies:
            copy.start()
        for copy in copies:
            copy.wait()

    return pl.pallas_call(
        kernel,
        out_shape=[jax.ShapeDtypeStruct((n, features), sources[0].dtype) for n in outs],
        in_specs=[pl.BlockSpec(memory_space=pl.ANY)] * len(sources),
        out_specs=[pl.BlockSpec(memory_space=pltpu.VMEM)] * len(outs),
        scratch_shapes=[pltpu.SemaphoreType.DMA((len(moves),))],
        compiler_params=pltpu.CompilerParams(vmem_limit_bytes=limit),
        cost_estimate=SMALL,
        name=name,
    )(*sources)


def table_rows(step, gate_table, gate_slope):
    features = gate_table.shape[1]

    def kernel(step, gate, slope, gate_row, slope_row):
        row = pl.ds(step[0] & 7, 1)
        gate_row[...] = gate[row, :]
        slope_row[...] = slope[row, :]

    table = pl.BlockSpec((8, features), lambda i, step: (step[0] >> 3, 0))
    one = pl.BlockSpec((1, features), lambda i, step: (0, 0))
    return pl.pallas_call(
        kernel,
        out_shape=[jax.ShapeDtypeStruct((1, features), gate_table.dtype)] * 2,
        grid_spec=pltpu.PrefetchScalarGridSpec(
            num_scalar_prefetch=1, grid=(1,), in_specs=[table, table], out_specs=[one, one]
        ),
        compiler_params=pltpu.CompilerParams(vmem_limit_bytes=VMEM_LIMIT),
        cost_estimate=SMALL,
        name="table_rows",
    )(step, gate_table, gate_slope)


def score_kernel(q, qt, k, kt, k_par, par, near_a, near_b, late_a, late_b, p_out, w_out):
    tokens, features = q.shape
    edge = near_a.shape[0] // 4
    half = 2 * edge
    inner = tokens - 2 * edge
    scaling = 1.0 / math.sqrt(HD)
    tm = lax.axis_index("tm")
    inside = (tm > 0) & (tm < lax.axis_size("tm") - 1)
    seen = jnp.where(inside, tokens + 2 * half + inner + half, tokens + 2 * half + inner)
    allowed = lax.broadcasted_iota(jnp.int32, (tokens, 2 * tokens + 2 * half), 1) < seen
    for head in range(features // HD):
        at = pl.ds(head * HD, HD)

        def ordered(own, par, i):
            rows = pl.ds(i * edge, edge)
            return jnp.concatenate(
                [
                    own[:, at],
                    par[pl.ds(0, edge), at],
                    par[pl.ds(tokens - edge, edge), at],
                    near_a[rows, at],
                    late_a[rows, at],
                    par[pl.ds(edge, inner), at],
                    near_b[rows, at],
                    late_b[rows, at],
                ],
                0,
            )

        keys, keys_t = ordered(k, k_par, 0), ordered(kt, par, 1)
        query, query_t = q[:, at], qt[:, at]
        raw = jnp.where(allowed, dot_nt(query, keys), -1e30)
        top = jnp.max(raw, axis=-1, keepdims=True)
        lifted = jnp.exp2((raw - top) * (scaling * LOG2E))
        probs = lifted * (1.0 / jnp.sum(lifted, axis=-1, keepdims=True))
        slopes = scaling * dot_nt(
            jnp.concatenate([query_t, query], 1), jnp.concatenate([keys, keys_t], 1)
        )
        centre = jnp.sum(probs * slopes, axis=-1, keepdims=True)
        probs_low = probs.astype(jnp.bfloat16)
        weights_t = (probs * (slopes - centre)).astype(jnp.bfloat16)
        p_out[head] = probs_low
        w_out[head] = weights_t


def scores(*arrays):
    tokens, features = arrays[0].shape
    heads = features // HD
    keys = 2 * tokens + arrays[-1].shape[0]
    out = jax.ShapeDtypeStruct((heads, tokens, keys), jnp.bfloat16)
    return pl.pallas_call(
        score_kernel,
        out_shape=(out, out),
        in_specs=[pl.BlockSpec(memory_space=pltpu.VMEM)] * len(arrays),
        out_specs=[pl.BlockSpec(memory_space=pltpu.VMEM)] * 2,
        compiler_params=pltpu.CompilerParams(vmem_limit_bytes=VMEM_LIMIT),
        cost_estimate=SCORES_COST,
        name="scores",
    )(*arrays)


def finish_kernel(layout, gate, slope, p, w, own, mids, par, near_a, near_b, late_a, late_b, v_mid, *rest):
    pieces = rest[: len(layout)]
    out_p, out_t, weight, attn, rounded, sems = rest[len(layout) :]
    tokens = p.shape[1]
    edge = near_a.shape[0] // 4
    half, inner = 2 * edge, tokens - 2 * edge
    for head in range(p.shape[0]):
        at = pl.ds(head * HD, HD)

        def ordered(i):
            halo = pl.ds(half + i * edge, edge)
            base = tokens + i * half
            return jnp.concatenate(
                [
                    own[pl.ds(base, edge), at],
                    mids[pl.ds(i * inner, inner), at],
                    own[pl.ds(base + edge, edge), at],
                    par[pl.ds(base, half), at],
                    near_a[halo, at],
                    late_a[halo, at],
                    v_mid[pl.ds(i * inner, inner), at],
                    near_b[halo, at],
                    late_b[halo, at],
                ],
                0,
            )

        values, values_t = ordered(0), ordered(1)
        probs = p[head]
        primal = jnp.dot(probs, values, preferred_element_type=jnp.float32)
        tangent = jnp.dot(
            jnp.concatenate([w[head], probs], 1),
            jnp.concatenate([values, values_t], 0),
            preferred_element_type=jnp.float32,
        )
        attn[pl.ds(0, tokens), at] = primal.astype(jnp.bfloat16)
        attn[pl.ds(tokens, tokens), at] = tangent.astype(jnp.bfloat16)
    tm, h, f = (lax.axis_index(axis) for axis in ("tm", "height", "fsdp"))
    for piece, (units, rows) in zip(pieces, layout):
        for i, unit in enumerate(units):
            start = 0
            if unit is not None:
                dh, df, dq = unit
                wide = weight.shape[0] // (lax.axis_size("height") * lax.axis_size("fsdp"))
                start = ((h ^ dh) * lax.axis_size("fsdp") + (f ^ df)) * wide
                if dq is not None:
                    start = start + ((tm & 3) ^ dq) * rows
                start = pl.multiple_of(start, 16)
            weight[pl.ds(start, rows), :] = piece[pl.ds(i * rows, rows), :]
    width = 256
    copies = []
    for step, first in enumerate(range(0, weight.shape[0], width)):
        cols = pl.ds(first, width)
        both = dot_nt(attn[...], weight[cols, :])
        main, main_t = both[:tokens], both[tokens:]
        gate_row, slope_row = gate[:, cols], slope[:, cols]
        rounded[0, :, cols] = (gate_row * main).astype(jnp.bfloat16)
        rounded[1, :, cols] = (gate_row * main_t + slope_row * main).astype(jnp.bfloat16)
        for i, out in enumerate((out_p, out_t)):
            copies.append(pltpu.make_async_copy(rounded.at[i, :, cols], out.at[:, cols], sems.at[step, i]))
            copies[-1].start()
    for copy in copies:
        copy.wait()


def finish(gate, slope, probs, weights_t, values, pieces, layout):
    tokens, features = probs.shape[1], values[0].shape[1]
    dout = gate.shape[1]
    arrays = (gate, slope, probs, weights_t, *values, *pieces)
    out = jax.ShapeDtypeStruct((tokens, dout), jnp.bfloat16)
    return pl.pallas_call(
        lambda *refs: finish_kernel(layout, *refs),
        out_shape=(out, out),
        in_specs=[pl.BlockSpec(memory_space=pltpu.VMEM)] * len(arrays),
        out_specs=[pl.BlockSpec(memory_space=pl.ANY)] * 2,
        scratch_shapes=[
            pltpu.VMEM((dout, features), jnp.bfloat16),
            pltpu.VMEM((2 * tokens, features), jnp.bfloat16),
            pltpu.VMEM((2, tokens, dout), jnp.bfloat16),
            pltpu.SemaphoreType.DMA((dout // 256, 2)),
        ],
        compiler_params=pltpu.CompilerParams(vmem_limit_bytes=VMEM_LIMIT),
        cost_estimate=SMALL,
        name="finish",
    )(*arrays)


def local(
    query_primal,
    key_primal,
    value_primal,
    query_tangent,
    key_tangent,
    value_tangent,
    out_weight,
    gate_table,
    gate_slope,
    timestep,
):
    _, frames, rows, columns, features = query_primal.shape
    per_frame = rows * columns
    tokens = frames * per_frame
    flat = lambda x: x.reshape(tokens, features)
    q, qt, k, kt, v, vt = map(
        flat, (query_primal, query_tangent, key_primal, key_tangent, value_primal, value_tangent)
    )
    block = out_weight.T
    wide = block.shape[0]
    part = wide // 4
    fsdp = lax.axis_size("fsdp")
    in_quarters = (lax.axis_size("tm") % 4, lax.axis_size("height"), fsdp) == (0, 2, 4) and part % 16 == 0
    two = 2 * per_frame
    inner, last = tokens - two, tokens - per_frame
    ends = ((0, last), (last, 0))

    def own_parts(k, kt, v, vt):
        moves = [(1, 0, 0, 0, tokens)]
        for i, source in ((0, 2), (1, 3)):
            moves.append((source, 0, 0, tokens + i * two, per_frame))
            moves.append((source, last, 0, tokens + i * two + per_frame, per_frame))
            moves.append((source, per_frame, 1, inner * i, inner))
        for out, (odd, even) in ((2, ends[0]), (3, ends[1])):
            for source in range(4):
                moves.append((source, (even, odd), out, source * per_frame, per_frame))
        return gather_rows("own_parts", [tokens + 2 * two, 2 * inner, 2 * two, 2 * two], moves, [k, kt, v, vt], 58 * 1024 * 1024)

    def late_parts(k_par, par):
        moves = []
        for out, (odd, even) in ((0, ends[0]), (1, ends[1])):
            for i in range(2):
                moves.append((i, (even, odd), out, i * per_frame, per_frame))
                row = tuple(tokens + i * two + min(end, per_frame) for end in (even, odd))
                moves.append((1, row, out, (2 + i) * per_frame, per_frame))
        return gather_rows("late_parts", [2 * two, 2 * two], moves, [k_par, par])

    steps = {
        "k": ((), lambda: k),
        "kt": ((), lambda: kt),
        "v": ((), lambda: (v, vt)),
        "own_parts": (("k", "kt", "v"), lambda k, kt, v: own_parts(k, kt, *v)),
        "k_par": (("k",), lambda k: swap(k, "height", 1)),
        "par": (("own_parts",), lambda parts: swap(parts[0], "height", 1)),
        "v_mid": (("own_parts",), lambda parts: swap(parts[1], "height", 1)),
        "near_a": (("own_parts",), lambda parts: swap(parts[2], "tm", 1)),
        "near_b": (("own_parts",), lambda parts: swap_odd_alone(parts[3], "tm")),
        "late_parts": (("k_par", "par"), late_parts),
        "late_a": (("late_parts",), lambda sides: swap(sides[0], "tm", 1)),
        "late_b": (("late_parts",), lambda sides: swap_odd(sides[1], False)),
        "scores": (
            ("k_par", "par", "near_a", "near_b", "late_a", "late_b"),
            lambda *arrays: scores(q, qt, k, kt, *arrays),
        ),
        "tables": ((), lambda: (timestep, gate_table, gate_slope)),
        "gates": (("tables",), lambda tables: table_rows(*tables)),
    }
    if in_quarters:
        mine = lax.axis_index("tm") & 3
        quarter = lambda which: lax.dynamic_slice_in_dim(block, which * part, part, 0)
        near = lambda group: [(dh, df, dq ^ 1) for dh, df, dq in group]
        cat = lambda *arrays: jnp.concatenate(arrays, 0)
        steps["own"] = ((), lambda: quarter(mine))
        steps["other"] = (("own",), lambda own: swap(own, "height", 1))
        steps["pair"] = (("own", "other"), cat)
        steps["half"] = (("pair",), lambda pair: cat(quarter(mine ^ 2), pair))
        steps["twos"] = (("pair",), lambda pair: swap(pair, "fsdp", 2))
        steps["ones"] = (("half",), lambda half: swap(half, "fsdp", 1))
        steps["threes"] = (("twos", "other_x"), lambda *units: swap(cat(*units), "fsdp", 1))
        steps["other_x"] = (("other",), lambda other: swap(other, "tm", 2))
        steps["cross"] = (("twos",), lambda twos: swap(twos, "tm", 2))
        steps["cross_threes"] = (("threes",), lambda threes: swap(threes[: 2 * part], "tm", 2))
        steps["mine"] = (("other", "ones", "twos", "threes", "other_x", "cross", "cross_threes"), cat)
        units = [(1, 0, 0), (0, 1, 2), (0, 1, 0), (1, 1, 0), (0, 2, 0), (1, 2, 0), (0, 3, 0), (1, 3, 0), (1, 1, 2)]
        units += [(1, 0, 2), (0, 2, 2), (1, 2, 2), (0, 3, 2), (1, 3, 2)]
        steps["near"] = (("mine",), lambda mine: swap(mine, "tm", 1))
        pieces = ("mine", "near")
        layout = [([(0, 0, None)], wide), (units, part), (near(units), part)]
        order = ORDER
    else:
        steps["weight"] = ((), lambda: lax.all_gather(block, ("height", "fsdp"), axis=0, tiled=True))
        pieces, layout, order = ("weight",), [([None], gate_table.shape[1])], {}
    known = {}

    def get(name):
        if name not in known:
            takes, make = steps[name]
            arrays = [get(take) for take in takes]
            first = [get(step) for step in order.get(name, ())]
            if first:
                arrays = lax.optimization_barrier((arrays, first))[0]
            known[name] = make(*arrays)
        return known[name]

    probs, weights_t = get("scores")
    own, middle, _, _ = get("own_parts")
    values = (own, middle, *(get(name) for name in ("par", "near_a", "near_b", "late_a", "late_b", "v_mid")))
    parts = ([block] if in_quarters else []) + [get(piece) for piece in pieces]
    out_p, out_t = finish(*get("gates"), probs, weights_t, values, parts, layout)
    shape = query_primal.shape[:-1] + (out_p.shape[1],)
    return out_p.reshape(shape), out_t.reshape(shape)


def solution(mesh):
    token_spec = P("fsdp", "tm", "height", None, None)
    in_specs = (token_spec,) * 6 + (P(None, ("height", "fsdp")), P(), P(), P("fsdp"))
    return jax.shard_map(
        local, mesh=mesh, in_specs=in_specs, out_specs=(token_spec, token_spec), check_vma=False
    )
```
